32 devices in a mesh: client: 8 (over z, x), shard: 4 (over y, core).
Axes of the slice: x: 2, y: 2, z: 4, core: 2. Of those that a mesh axis runs over, the one named last changes fastest.
Arguments:
- delta: bfloat16 [8, 4096, 14336], P('client', 'shard'), may hold values from -750 to 750
- start_coeffs: bfloat16 [14336, 64], replicated, may hold values from -0.046875 to 0.046875
- noise_p: float32 [2, 4096, 64], P(None, 'shard'), may hold values from -6 to 6
- noise_q: float32 [2, 14336, 64], P(None, 'shard'), may hold values from -6 to 6
Outputs:
- basis: float32 [4096, 64], P('shard')
- coeffs: float32 [14336, 64], P('shard')
The draws below stay inside these ranges and needn't reach their ends.
All inputs are finite; a program needn't handle non-finite values.
Results may differ from the reference program's by a relative error of at most 0.0033.
Values may be sent and summed in bfloat16 or wider, within the bound.
A program may use at most 128 MiB of HBM per device.

```python
import math
import jax
import jax.numpy as jnp
from jax import lax

D = 4096
FF = 14336
R = 64
ITERS = 2
CLIENTS = 8


def draw_delta(key, part):
    first, second, third, fourth = jax.random.split(key, 4)
    base = jax.random.truncated_normal(first, -4.0, 4.0, (CLIENTS, D, FF), jnp.float32)
    top = math.log(10.0)
    slope = 2.0
    quiet_gain = 0.007
    row_scale = jnp.exp(top * jax.random.uniform(second, (CLIENTS, D, 1), jnp.float32))
    col_scale = jnp.exp(top * jax.random.uniform(third, (CLIENTS, 1, FF), jnp.float32))
    trend = jnp.sqrt(1.0 + slope * jnp.arange(D, dtype=jnp.float32) / D)[None, :, None]
    quiet_count = max(2, CLIENTS // 5)
    order = jax.random.permutation(fourth, CLIENTS)
    client_gain = jnp.where(order < quiet_count, jnp.float32(quiet_gain), jnp.float32(1.0))[:, None, None]
    return (base * row_scale * col_scale * trend * client_gain).astype(jnp.bfloat16)


def level_of(rng, extent, cuts, least, largest):
    loudness = 1.0
    for dim, parts in cuts:
        heights = jax.random.uniform(jax.random.fold_in(jax.random.fold_in(rng, 6), dim), (parts,), jnp.float32, least / len(cuts), largest / len(cuts))
        loudness = loudness * jnp.repeat(jnp.exp(heights), extent[dim] // parts).reshape((-1,) + (1,) * (len(extent) - 1 - dim))
    return loudness


def bell_draw(key, dims, width, reach, cuts=(), held_as=jnp.bfloat16):
    array = width * jax.random.normal(key, dims, jnp.float32)
    if cuts:
        array = array * level_of(key, dims, cuts, -0.22, 0.18)
    return jnp.clip(array, -reach, reach).astype(held_as)


def setup_inputs(seed: int = 0) -> dict:
    arg_keys = jax.random.split(jax.random.key(seed), 5)
    delta = draw_delta(jax.random.fold_in(arg_keys[4], 71), 0)
    start_coeffs = bell_draw(arg_keys[1], (FF, R), FF ** -0.5, 0.046875)
    noise_p = bell_draw(arg_keys[2], (ITERS, D, R), 1.0, 6.0, ((1, 4),), jnp.float32)
    noise_q = bell_draw(arg_keys[3], (ITERS, FF, R), 1.0, 6.0, ((1, 4),), jnp.float32)
    return dict(delta=delta, start_coeffs=start_coeffs, noise_p=noise_p, noise_q=noise_q)


EPS = 1e-06
CLIP_FRACTION = 0.5

def reference(delta, start_coeffs, noise_p, noise_q):

    def square_sum(carry, matrix):
        return (carry, jnp.sum(jnp.square(matrix.astype(jnp.float32))))
    _, sumsq = lax.scan(square_sum, jnp.float32(0.0), delta)
    scale = jnp.minimum(1.0, CLIP_FRACTION * math.sqrt(D * FF) / jnp.sqrt(sumsq + EPS))
    coeffs = start_coeffs.astype(jnp.float32)
    panel = jnp.zeros((D, R), jnp.float32)
    for step in range(ITERS):
        qb = coeffs.astype(jnp.bfloat16)
        level = jnp.sqrt(jnp.sum(jnp.square(coeffs)) / R)

        def add_panel(total, item):
            matrix, factor = item
            return (total + factor * jnp.dot(matrix.astype(jnp.float32), qb.astype(jnp.float32), preferred_element_type=jnp.float32), None)
        panel, _ = lax.scan(add_panel, jnp.zeros((D, R), jnp.float32), (delta, scale))
        panel = panel + level * noise_p[step]
        gram = jnp.dot(panel.T.astype(jnp.float32), panel.astype(jnp.float32), precision=lax.Precision.HIGHEST, preferred_element_type=jnp.float32)
        lower = jnp.linalg.cholesky(gram)
        panel = jax.scipy.linalg.solve_triangular(lower, panel.T, lower=True).T
        pb = panel.astype(jnp.bfloat16)

        def add_coeffs(total, item):
            matrix, factor = item
            return (total + factor * jnp.dot(matrix.T.astype(jnp.float32), pb.astype(jnp.float32), preferred_element_type=jnp.float32), None)
        coeffs, _ = lax.scan(add_coeffs, jnp.zeros((FF, R), jnp.float32), (delta, scale))
        coeffs = coeffs + noise_q[step]
    return (math.sqrt(D) * panel, coeffs)
```

```python
import functools
import math

import jax
import jax.numpy as jnp
from jax import lax
from jax.experimental import pallas as pl
from jax.experimental.pallas import tpu as pltpu
from jax.sharding import PartitionSpec as P

ITERS = 2
EPS = 1e-06
CLIP_FRACTION = 0.5
LANES = 128
MESH = pl.DeviceIdType.MESH
F32 = jnp.float32
BF16 = jnp.bfloat16
HIGH = lax.Precision.HIGHEST


def nt(a, b, precision=None):
    return lax.dot_general(
        a, b, (((1,), (1,)), ((), ())), precision=precision, preferred_element_type=F32
    )


def inverse_lower(gram):
    n = gram.shape[0]
    rows = lax.broadcasted_iota(jnp.int32, (n, n), 0)
    cols = lax.broadcasted_iota(jnp.int32, (n, n), 1)
    work = jnp.concatenate([gram, (rows == cols).astype(F32)], axis=1)
    at = lax.broadcasted_iota(jnp.int32, (n, 2 * n), 0)
    out = jnp.zeros((n, 2 * n), F32)
    for j in range(n):
        row = work[j : j + 1, :]
        root = 1.0 / jnp.sqrt(row[:, j : j + 1])
        row = row * root
        out = jnp.where(at == j, row, out)
        if j < n - 1:
            work = work - (work[:, j : j + 1] * root) * row
    return out[:, n:]


def kernel(
    sizes, delta_hbm, start, noise_p, noise_q, basis_ref, coeffs_ref,
    delta, acc, sq_buf, sq_all, p_send, p_recv, p_own, p_all, g_buf, pb,
    core_send, core_recv, own, y_send, y_recv, z_send, z_recv, q_own, q_piece, q_all,
    l_own, l_client, l_part, l_shard,
    load_sem, small_send, small_recv, p_sems, g_sems, core_sems, y_sems, z_sems,
    a_sems, ay_sems, ac_sems, lc_sems, ls_sems,
):
    clients, shards, sub, units, unit, chunks = sizes
    ys = shards // 2
    rows, full = delta.shape
    rank = start.shape[1]
    piece = rows // clients
    wide = sub * LANES
    span = units * wide
    me_c = lax.axis_index("client")
    me_s = lax.axis_index("shard")
    core = lax.rem(me_s, 2)
    me_y = me_s // 2

    chunk = full // chunks

    def load(i):
        return pltpu.make_async_copy(
            delta_hbm.at[0, :, pl.ds(i * chunk, chunk)],
            delta.at[:, pl.ds(i * chunk, chunk)],
            load_sem.at[i],
        )

    for i in range(chunks):
        load(i).start()

    barrier = pltpu.get_barrier_semaphore()
    for d in range(1, clients):
        pl.semaphore_signal(
            barrier, inc=1, device_id=(lax.rem(me_c + d, clients), me_s), device_id_type=MESH
        )
    for d in range(1, shards):
        pl.semaphore_signal(
            barrier, inc=1, device_id=(me_c, lax.rem(me_s + d, shards)), device_id_type=MESH
        )

    def send(src, dst, sems, index, device):
        return pltpu.make_async_remote_copy(
            src_ref=src, dst_ref=dst,
            send_sem=sems.at[(0,) + index], recv_sem=sems.at[(1,) + index],
            device_id=device, device_id_type=MESH,
        )

    def to_client(d):
        return (lax.rem(me_c + d, clients), me_s)

    def to_shard(d):
        return (me_c, lax.rem(me_s + d, shards))

    def start_sum(i, total):
        v = start[pl.ds(pl.multiple_of(i * wide, wide), wide), :].astype(F32)
        return total + jnp.sum(v * v, axis=0, keepdims=True)

    level0 = jnp.sqrt(
        jnp.sum(lax.fori_loop(0, full // wide, start_sum, jnp.zeros((1, rank), F32)), axis=1, keepdims=True)
        / rank
    )

    acc[...] = jnp.zeros_like(acc)
    step = 512
    total = jnp.zeros((8, step), F32)
    for i in range(chunks):
        load(i).wait()

        def first(j, total, i=i):
            at = pl.multiple_of(i * chunk + j * step, step)
            acc[...] += jnp.dot(
                delta[:, pl.ds(at, step)], start[pl.ds(at, step), :], preferred_element_type=F32
            )

            def squares(r, t):
                v = delta[pl.ds(pl.multiple_of(r * 128, 128), 128), pl.ds(at, step)].astype(F32)
                return t + jnp.sum((v * v).reshape(16, 8, step), axis=0)

            return lax.fori_loop(0, rows // 128, squares, total)

        total = lax.fori_loop(0, chunk // step, first, total)

    pl.semaphore_wait(barrier, clients + shards - 2)

    mine = jnp.sum(jnp.sum(total, axis=0, keepdims=True), axis=1, keepdims=True)
    sq_buf[...] = jnp.broadcast_to(mine, (8, LANES))
    for d in range(1, shards):
        pltpu.make_async_remote_copy(
            src_ref=sq_buf, dst_ref=sq_all.at[d - 1],
            send_sem=small_send.at[d - 1], recv_sem=small_recv.at[d - 1],
            device_id=to_shard(d), device_id_type=MESH,
        ).start()
    sumsq = sq_buf[0:1, 0:1]
    for d in range(1, shards):
        c = pltpu.make_async_remote_copy(
            src_ref=sq_buf, dst_ref=sq_all.at[d - 1],
            send_sem=small_send.at[d - 1], recv_sem=small_recv.at[d - 1],
            device_id=to_shard(d), device_id_type=MESH,
        )
        c.wait()
        sumsq = sumsq + sq_all[d - 1, 0:1, 0:1]
    count = rows * shards * full
    factor = jnp.minimum(1.0, CLIP_FRACTION * math.sqrt(count) / jnp.sqrt(sumsq + EPS))

    for it in range(ITERS):
        if it == 0:
            level = level0
        else:
            acc[...] = jnp.zeros_like(acc)

            def again(n, _):
                b = n // units
                k = lax.rem(n, units)
                at = pl.multiple_of(b * span + k * wide, LANES)
                v = q_all[b, k].astype(F32).reshape(sub * rank, LANES)
                v = jnp.concatenate([v[t * rank : (t + 1) * rank] for t in range(sub)], axis=1)
                acc[...] += nt(delta[:, pl.ds(at, wide)], v.astype(BF16))
                return 0

            lax.fori_loop(0, shards * units, again, 0)

        for d in range(clients):
            c = lax.rem(me_c + d, clients)
            v = acc[pl.ds(pl.multiple_of(c * piece, piece), piece), :] * factor
            p_send[it, d] = v.T
        copies = [
            send(p_send.at[it, d], p_recv.at[it, d], p_sems, (it, 0, d), to_client(d))
            for d in range(1, clients)
        ]
        for c in copies:
            c.start()
        v = p_send[it, 0] + level * noise_p[it]
        for d, c in enumerate(copies, 1):
            c.wait()
            v = v + p_recv[it, d]
        p_own[it] = v
        copies = [
            send(p_own.at[it], p_all.at[it, me_c], p_sems, (it, 1, d), to_client(d))
            for d in range(1, clients)
        ]
        for c in copies:
            c.start()
        p_all[it, me_c] = v
        for c in copies:
            c.wait()

        gram = jnp.zeros((rank, rank), F32)
        for c in range(clients):
            v = p_all[it, c]
            gram = gram + nt(v, v, HIGH)
        g_buf[it, 0] = gram
        copies = [
            send(g_buf.at[it, 0], g_buf.at[it, d], g_sems, (it, d), to_shard(d))
            for d in range(1, shards)
        ]
        for c in copies:
            c.start()
        for d, c in enumerate(copies, 1):
            c.wait()
            gram = gram + g_buf[it, d]
        inverse = inverse_lower(gram)
        for c in range(clients):
            v = jnp.dot(inverse, p_all[it, c], precision=HIGH, preferred_element_type=F32)
            pb[:, c * piece : (c + 1) * piece] = v.astype(BF16)
            if it == ITERS - 1:
                basis_ref[c] = v * math.sqrt(rows * shards)

        def block(owner, k):
            at = pl.multiple_of(owner * span + k * wide, LANES)
            v = factor * jnp.dot(pb[...], delta[:, pl.ds(at, wide)], preferred_element_type=F32)
            v = jnp.concatenate([v[:, t * LANES : (t + 1) * LANES] for t in range(sub)], axis=0)
            return v.reshape(clients, unit, LANES)

        sends = []
        y_copies = []
        for dy in list(range(1, ys)) + [0]:
            to_y = lax.rem(me_y + dy, ys)

            def other(k, _, to_y=to_y, dy=dy):
                core_send[it, dy, k] = block(2 * to_y + 1 - core, k)
                return 0

            lax.fori_loop(0, units, other, 0)
            c = send(core_send.at[it, dy], core_recv.at[it, dy], core_sems, (it, dy), (me_c, 2 * me_y + 1 - core))
            c.start()

            def same(k, _, to_y=to_y):
                own[k] = block(2 * to_y + core, k)
                return 0

            lax.fori_loop(0, units, same, 0)
            c.wait()
            if dy > 0:

                def add(k, _, dy=dy):
                    y_send[it, dy - 1, k] = (own[k] + core_recv[it, dy, k]).astype(BF16)
                    return 0

                lax.fori_loop(0, units, add, 0)
                c = send(y_send.at[it, dy - 1], y_recv.at[it, dy - 1], y_sems, (it, dy - 1), (me_c, 2 * to_y + core))
                c.start()
                y_copies.append(c)
        for c in y_copies:
            c.wait()

        def add_z(k, _):
            v = own[k] + core_recv[it, 0, k]
            for d in range(1, ys):
                v = v + y_recv[it, d - 1, k].astype(F32)
            own[k] = v
            for c in range(clients):
                z_send[it, c, k] = v[c].astype(BF16)
            return 0

        lax.fori_loop(0, units, add_z, 0)
        copies = [
            send(z_send.at[it, lax.rem(me_c + d, clients)], z_recv.at[it, d], z_sems, (it, d), to_client(d))
            for d in range(1, clients)
        ]
        for c in copies:
            c.start()
        for c in copies:
            c.wait()

        if it < ITERS - 1:
            square = jnp.zeros((1, LANES), F32)
            for k in range(units):
                v = own[k, me_c] + noise_q[k]
                for d in range(1, clients):
                    v = v + z_recv[it, d, k].astype(F32)
                q_piece[k] = v.astype(BF16)
                square = square + jnp.sum(v * v, axis=0, keepdims=True)
            part = jnp.sum(square, axis=1, keepdims=True)
            l_own[...] = jnp.broadcast_to(part, (8, LANES))
            q_all[me_s, :, me_c] = q_piece[...]
            copies = [
                send(q_piece, q_all.at[me_s, :, me_c], a_sems, (d,), to_client(d))
                for d in range(1, clients)
            ]
            l_copies = [send(l_own, l_client.at[d - 1], lc_sems, (d,), to_client(d)) for d in range(1, clients)]
            for c in copies + l_copies:
                c.start()
            later = []

            def pass_on(d):
                who = lax.rem(me_c + clients - d, clients)
                here = q_all.at[me_s, :, who]
                for dy in range(1, ys):
                    c = send(here, here, ay_sems, (d, dy - 1), (me_c, 2 * lax.rem(me_y + dy, ys) + core))
                    c.start()
                    later.append(c)
                c = send(here, here, ac_sems, (d, 0), (me_c, 2 * me_y + 1 - core))
                c.start()
                later.append(c)

            pass_on(0)
            for d, c in enumerate(copies, 1):
                c.wait_recv()
                pass_on(d)
            for d, c in enumerate(l_copies, 1):
                c.wait()
                part = part + l_client[d - 1, 0:1, 0:1]
            l_part[...] = jnp.broadcast_to(part, (8, LANES))
            l_copies = [send(l_part, l_shard.at[d - 1], ls_sems, (d,), to_shard(d)) for d in range(1, shards)]
            for c in l_copies:
                c.start()
            for d in range(clients):
                who = lax.rem(me_c + clients - d, clients)
                for dy in range(1, ys):
                    from_s = 2 * lax.rem(me_y + ys - dy, ys) + core
                    here = q_all.at[from_s, :, who]
                    send(here, here, ay_sems, (d, dy - 1), (me_c, me_s)).wait_recv()
                    c = send(here, here, ac_sems, (d, dy), (me_c, 2 * me_y + 1 - core))
                    c.start()
                    sends.append(c)
            for d in range(clients):
                who = lax.rem(me_c + clients - d, clients)
                for dy in range(ys):
                    from_s = 2 * lax.rem(me_y + ys - dy, ys) + 1 - core
                    here = q_all.at[from_s, :, who]
                    send(here, here, ac_sems, (d, dy), (me_c, me_s)).wait_recv()
            for c in later + sends + copies:
                c.wait_send()
            for d, c in enumerate(l_copies, 1):
                c.wait()
                part = part + l_shard[d - 1, 0:1, 0:1]
            level = jnp.sqrt(part / rank)
        else:
            for k in range(units):
                v = own[k, me_c]
                for d in range(1, clients):
                    v = v + z_recv[it, d, k].astype(F32)
                q_own[k] = v
            coeffs_ref[:, me_c] = q_own[...]
            copies = [
                send(q_own, coeffs_ref.at[:, me_c], a_sems, (clients + d,), to_client(d))
                for d in range(1, clients)
            ]
            for c in copies:
                c.start()
            for c in copies:
                c.wait()


def on_device(clients, shards, delta, start_coeffs, noise_p, noise_q):
    rows, full = delta.shape[1:]
    rank = start_coeffs.shape[1]
    ys = shards // 2
    piece = rows // clients
    tiles = full // shards // LANES
    sub = next(
        s for s in range(1, tiles + 1)
        if tiles % s == 0 and (s * rank) % (8 * clients) == 0 and s * rank >= 32 * clients
    )
    units = tiles // sub
    unit = sub * rank // clients
    chunks = 7
    me = lax.axis_index("client")

    own_p = lax.dynamic_slice_in_dim(noise_p, me * piece, piece, axis=1).transpose(0, 2, 1)
    slabs = noise_q.reshape(ITERS, units, sub, LANES, rank).transpose(0, 1, 2, 4, 3)
    slabs = slabs.reshape(ITERS, units, clients, unit, LANES)
    own_q = lax.dynamic_index_in_dim(slabs[0], me, axis=1, keepdims=False)

    dma = pltpu.SemaphoreType.DMA
    basis, coeffs = pl.pallas_call(
        functools.partial(kernel, (clients, shards, sub, units, unit, chunks)),
        out_shape=(
            jax.ShapeDtypeStruct((clients, rank, piece), F32),
            jax.ShapeDtypeStruct((units, clients, unit, LANES), F32),
        ),
        in_specs=[pl.BlockSpec(memory_space=pl.ANY)] + [pl.BlockSpec(memory_space=pltpu.VMEM)] * 3,
        out_specs=[pl.BlockSpec(memory_space=pltpu.VMEM)] * 2,
        scratch_shapes=[
            pltpu.VMEM((rows, full), BF16),
            pltpu.VMEM((rows, rank), F32),
            pltpu.VMEM((8, LANES), F32),
            pltpu.VMEM((shards - 1, 8, LANES), F32),
            pltpu.VMEM((ITERS, clients, rank, piece), F32),
            pltpu.VMEM((ITERS, clients, rank, piece), F32),
            pltpu.VMEM((ITERS, rank, piece), F32),
            pltpu.VMEM((ITERS, clients, rank, piece), F32),
            pltpu.VMEM((ITERS, shards, rank, rank), F32),
            pltpu.VMEM((rank, rows), BF16),
            pltpu.VMEM((ITERS, ys, units, clients, unit, LANES), F32),
            pltpu.VMEM((ITERS, ys, units, clients, unit, LANES), F32),
            pltpu.VMEM((units, clients, unit, LANES), F32),
            pltpu.VMEM((ITERS, ys - 1, units, clients, unit, LANES), BF16),
            pltpu.VMEM((ITERS, ys - 1, units, clients, unit, LANES), BF16),
            pltpu.VMEM((ITERS, clients, units, unit, LANES), BF16),
            pltpu.VMEM((ITERS, clients, units, unit, LANES), BF16),
            pltpu.VMEM((units, unit, LANES), F32),
            pltpu.VMEM((units, unit, LANES), BF16),
            pltpu.VMEM((shards, units, clients, unit, LANES), BF16),
            pltpu.VMEM((8, LANES), F32),
            pltpu.VMEM((clients - 1, 8, LANES), F32),
            pltpu.VMEM((8, LANES), F32),
            pltpu.VMEM((shards - 1, 8, LANES), F32),
            dma((chunks,)),
            dma((shards - 1,)),
            dma((shards - 1,)),
            dma((2, ITERS, 2, clients)),
            dma((2, ITERS, shards)),
            dma((2, ITERS, ys)),
            dma((2, ITERS, ys)),
            dma((2, ITERS, clients)),
            dma((2, 2 * clients)),
            dma((2, clients, ys)),
            dma((2, clients, ys)),
            dma((2, clients)),
            dma((2, shards)),
        ],
        compiler_params=pltpu.CompilerParams(
            collective_id=0, has_side_effects=True, vmem_limit_bytes=60 * 1024 * 1024
        ),
        cost_estimate=pl.CostEstimate(
            flops=8 * rows * full * rank, bytes_accessed=2 * rows * full, transcendentals=0
        ),
    )(delta, start_coeffs, own_p, own_q)
    basis = basis.transpose(0, 2, 1).reshape(rows, rank)
    coeffs = coeffs.reshape(units, sub, rank, LANES).transpose(0, 1, 3, 2).reshape(full // shards, rank)
    return basis, coeffs + noise_q[ITERS - 1]


def solution(mesh):
    placed = (P("client", "shard", None), P(), P(None, "shard", None), P(None, "shard", None))
    return jax.shard_map(
        functools.partial(on_device, mesh.shape["client"], mesh.shape["shard"]),
        mesh=mesh,
        in_specs=placed,
        out_specs=(P("shard", None), P("shard", None)),
        check_vma=False,
    )
```

```python
import functools
import math

import jax
import jax.numpy as jnp
from jax import lax
from jax.experimental import pallas as pl
from jax.experimental.pallas import tpu as pltpu
from jax.sharding import PartitionSpec as P

ITERS = 2
EPS = 1e-06
CLIP_FRACTION = 0.5
LANES = 128
MESH = pl.DeviceIdType.MESH
F32 = jnp.float32
BF16 = jnp.bfloat16
HIGH = lax.Precision.HIGHEST


def nt(a, b, precision=None):
    return lax.dot_general(
        a, b, (((1,), (1,)), ((), ())), precision=precision, preferred_element_type=F32
    )


def inverse_lower(gram):
    n = gram.shape[0]
    tall = 8
    rows = lax.broadcasted_iota(jnp.int32, (n, n), 0)
    cols = lax.broadcasted_iota(jnp.int32, (n, n), 1)
    eye = (rows == cols).astype(F32)
    work = jnp.concatenate([gram, eye], axis=1)
    work = [work[i : i + tall] for i in range(0, n, tall)]
    at = lax.broadcasted_iota(jnp.int32, (tall, 2 * n), 0)
    done = []
    for j in range(n):
        b, r = j // tall, j % tall
        row = work[b][r : r + 1]
        done.append(row if r == 0 else jnp.where(at == r, row, done.pop()))
        if r == 0:
            done[-1] = jnp.broadcast_to(row, (tall, 2 * n))
        step = row * (1.0 / row[:, j : j + 1])
        for i in range(b, n // tall):
            work[i] = work[i] - work[i][:, j : j + 1] * step
    done = jnp.concatenate(done, axis=0)
    pivots = jnp.sum(done[:, :n] * eye, axis=1, keepdims=True)
    return done[:, n:] * (1.0 / jnp.sqrt(pivots))


def kernel(
    sizes, delta_hbm, start_hbm, noise_p_hbm, noise_q_hbm, basis_ref, coeffs_ref,
    delta, start, noise_p, noise_q, slabs, acc, sq_buf, sq_all, p_send, p_recv, p_all, g_buf, pb,
    core_send, core_recv, own, y_send, y_recv, z_send, z_recv, q_all, q_last,
    l_own, l_client, l_part, l_shard,
    load_sem, extra_sem, small_send, small_recv, p_sems, g_sems, core_sems, y_sems, z_sems,
    a_sems, ax_sems, ay_sems, ac_sems, f_sems, fx_sems, lc_sems, ls_sems,
):
    clients, shards, minor, sub, units, unit, chunks, groups = sizes
    major = clients // minor
    ys = shards // 2
    rows, full = delta.shape
    rank = start.shape[0]
    piece = rows // clients
    wide = sub * LANES
    span = units * wide
    me_c = lax.axis_index("client")
    me_s = lax.axis_index("shard")
    me_a, me_b = me_c // minor, lax.rem(me_c, minor)
    core = lax.rem(me_s, 2)
    me_y = me_s // 2
    chunk = full // chunks

    def load(i):
        return pltpu.make_async_copy(
            delta_hbm.at[0, :, pl.ds(i * chunk, chunk)],
            delta.at[:, pl.ds(i * chunk, chunk)],
            load_sem.at[i],
        )

    if piece % LANES == 0:
        mine_p = noise_p_hbm.at[:, :, pl.ds(pl.multiple_of(me_c * piece, LANES), piece)]
    else:
        mine_p = noise_p_hbm
    extras = [
        pltpu.make_async_copy(start_hbm, start, extra_sem.at[0]),
        pltpu.make_async_copy(mine_p, noise_p, extra_sem.at[1]),
        pltpu.make_async_copy(noise_q_hbm.at[0], noise_q, extra_sem.at[2]),
    ]
    extras[0].start()
    for i in range(chunks):
        load(i).start()
    extras[1].start()
    extras[2].start()

    barrier = pltpu.get_barrier_semaphore()
    for d in range(1, clients):
        pl.semaphore_signal(
            barrier, inc=1, device_id=(lax.rem(me_c + d, clients), me_s), device_id_type=MESH
        )
    for d in range(1, shards):
        pl.semaphore_signal(
            barrier, inc=1, device_id=(me_c, lax.rem(me_s + d, shards)), device_id_type=MESH
        )

    def send(src, dst, sems, index, device):
        return pltpu.make_async_remote_copy(
            src_ref=src, dst_ref=dst,
            send_sem=sems.at[(0,) + index], recv_sem=sems.at[(1,) + index],
            device_id=device, device_id_type=MESH,
        )

    def to_client(d):
        return (lax.rem(me_c + d, clients), me_s)

    def to_shard(d):
        return (me_c, lax.rem(me_s + d, shards))

    def to_major(d):
        return (lax.rem(me_a + d, major) * minor + me_b, me_s)

    def to_minor(d):
        return (me_a * minor + lax.rem(me_b + d, minor), me_s)

    def came_from(da, db):
        return lax.rem(me_a + major - da, major) * minor + lax.rem(me_b + minor - db, minor)

    to_core = (me_c, 2 * me_y + 1 - core)

    def to_slabs(v):
        v = jnp.concatenate([v[:, t * LANES : (t + 1) * LANES] for t in range(sub)], axis=0)
        return v.reshape(clients, unit, LANES)

    def from_slabs(v):
        v = v.reshape(sub * rank, LANES)
        return jnp.concatenate([v[t * rank : (t + 1) * rank] for t in range(sub)], axis=1)

    extras[0].wait()

    def start_sum(i, total):
        v = start[:, pl.ds(pl.multiple_of(i * wide, LANES), wide)].astype(F32)
        return total + jnp.sum(v * v, axis=0, keepdims=True)

    level0 = jnp.sqrt(
        jnp.sum(lax.fori_loop(0, full // wide, start_sum, jnp.zeros((1, wide), F32)), axis=1, keepdims=True)
        / rank
    )

    acc[...] = jnp.zeros_like(acc)
    step = 512
    total = jnp.zeros((8, step), F32)
    for i in range(chunks):
        load(i).wait()

        def first(j, total, i=i):
            at = pl.multiple_of(i * chunk + j * step, step)
            acc[...] += nt(delta[:, pl.ds(at, step)], start[:, pl.ds(at, step)])

            def squares(r, t):
                v = delta[pl.ds(pl.multiple_of(r * 128, 128), 128), pl.ds(at, step)].astype(F32)
                return t + jnp.sum((v * v).reshape(16, 8, step), axis=0)

            return lax.fori_loop(0, rows // 128, squares, total)

        total = lax.fori_loop(0, chunk // step, first, total)

    pl.semaphore_wait(barrier, clients + shards - 2)

    mine = jnp.sum(jnp.sum(total, axis=0, keepdims=True), axis=1, keepdims=True)
    sq_buf[...] = jnp.broadcast_to(mine, (8, LANES))
    sq_copies = [
        pltpu.make_async_remote_copy(
            src_ref=sq_buf, dst_ref=sq_all.at[d - 1],
            send_sem=small_send.at[d - 1], recv_sem=small_recv.at[d - 1],
            device_id=to_shard(d), device_id_type=MESH,
        )
        for d in range(1, shards)
    ]
    for c in sq_copies:
        c.start()
    extras[1].wait()
    extras[2].wait()
    for k in range(units):
        slabs[k] = to_slabs(noise_q[:, k * wide : (k + 1) * wide])

    for it in range(ITERS):
        for d in range(clients):
            c = lax.rem(me_c + d, clients)
            v = acc[pl.ds(pl.multiple_of(c * piece, piece), piece), :]
            p_send[it, d] = v.T
        if it == 0:
            level = level0
            sumsq = sq_buf[0:1, 0:1]
            for d, c in enumerate(sq_copies, 1):
                c.wait()
                sumsq = sumsq + sq_all[d - 1, 0:1, 0:1]
            count = rows * shards * full
            factor = jnp.minimum(1.0, CLIP_FRACTION * math.sqrt(count) / jnp.sqrt(sumsq + EPS))
        copies = [
            send(p_send.at[it, d], p_recv.at[it, d], p_sems, (it, 0, d), to_client(d))
            for d in range(1, clients)
        ]
        for d, c in enumerate(copies, 1):
            p_send[it, d] = p_send[it, d] * factor
            c.start()
        v = p_send[it, 0] * factor + level * noise_p[it]
        for d, c in enumerate(copies, 1):
            c.wait()
            v = v + p_recv[it, d]
        p_all[it, me_c] = v
        copies = [
            send(p_all.at[it, me_c], p_all.at[it, me_c], p_sems, (it, 1, d), to_client(d))
            for d in range(1, clients)
        ]
        for c in copies:
            c.start()
        for c in copies:
            c.wait()

        panel = jnp.concatenate([p_all[it, c] for c in range(clients)], axis=1)
        gram = nt(panel, panel, HIGH)
        g_buf[it, 0] = gram
        copies = [
            send(g_buf.at[it, 0], g_buf.at[it, d], g_sems, (it, d), to_shard(d))
            for d in range(1, shards)
        ]
        for c in copies:
            c.start()
        for d, c in enumerate(copies, 1):
            c.wait()
            gram = gram + g_buf[it, d]
        panel = jnp.dot(inverse_lower(gram), panel, precision=HIGH, preferred_element_type=F32)
        pb[...] = panel.astype(BF16)
        if it == ITERS - 1:
            basis_ref[...] = panel

        def block(owner, k):
            at = pl.multiple_of(owner * span + k * wide, LANES)
            return to_slabs(factor * jnp.dot(pb[...], delta[:, pl.ds(at, wide)], preferred_element_type=F32))

        y_copies = []
        for dy in list(range(1, ys)) + [0]:
            to_y = lax.rem(me_y + dy, ys)
            core_copies = []
            for g, (k0, k1) in enumerate(groups):

                def other(k, _, to_y=to_y, dy=dy):
                    core_send[it, dy, k] = block(2 * to_y + 1 - core, k)
                    return 0

                lax.fori_loop(k0, k1, other, 0)
                part = pl.ds(k0, k1 - k0)
                c = send(core_send.at[it, dy, part], core_recv.at[it, dy, part], core_sems, (it, dy, g), to_core)
                c.start()
                core_copies.append(c)

            for g, (k0, k1) in enumerate(groups):

                def same(k, _, to_y=to_y):
                    own[k] = block(2 * to_y + core, k)
                    return 0

                def add_core(k, _, dy=dy):
                    v = own[k] + core_recv[it, dy, k]
                    if dy > 0:
                        y_send[it, dy - 1, k] = v.astype(BF16)
                    else:
                        own[k] = v
                    return 0

                lax.fori_loop(k0, k1, same, 0)
                core_copies[g].wait()
                lax.fori_loop(k0, k1, add_core, 0)
                if dy > 0:
                    part = pl.ds(k0, k1 - k0)
                    c = send(
                        y_send.at[it, dy - 1, part], y_recv.at[it, dy - 1, part],
                        y_sems, (it, dy, g), (me_c, 2 * to_y + core),
                    )
                    c.start()
                    y_copies.append((g, c))
        z_copies = []
        for g, (k0, k1) in enumerate(groups):
            for h, c in y_copies:
                if h == g:
                    c.wait()

            def add_y(k, _):
                v = own[k]
                for d in range(1, ys):
                    v = v + y_recv[it, d - 1, k].astype(F32)
                own[k] = v
                for c in range(clients):
                    z_send[it, c, k] = v[c].astype(BF16)
                return 0

            lax.fori_loop(k0, k1, add_y, 0)
            part = pl.ds(k0, k1 - k0)
            for d in range(1, clients):
                c = send(
                    z_send.at[it, lax.rem(me_c + d, clients), part], z_recv.at[it, d, part],
                    z_sems, (it, d, g), to_client(d),
                )
                c.start()
                z_copies.append((g, c))

        square = jnp.zeros((1, LANES), F32)
        for g, (k0, k1) in enumerate(groups):
            for h, c in z_copies:
                if h == g:
                    c.wait()
            for k in range(k0, k1):
                v = own[k, me_c]
                for d in range(1, clients):
                    v = v + z_recv[it, d, k].astype(F32)
                if it < ITERS - 1:
                    v = v + slabs[k, me_c]
                    square = square + jnp.sum(v * v, axis=0, keepdims=True)
                    q_all[me_s, k, me_c] = v.astype(BF16)
                else:
                    q_last[k, me_c] = v

        if it == ITERS - 1:
            here = q_last.at[:, me_c]
            copies = [send(here, here, f_sems, (d,), to_major(d)) for d in range(1, major)]
            for c in copies:
                c.start()
            passed = []
            for da in range(major):
                if da > 0:
                    copies[da - 1].wait_recv()
                here = q_last.at[:, came_from(da, 0)]
                for db in range(1, minor):
                    c = send(here, here, fx_sems, (da, db), to_minor(db))
                    c.start()
                    passed.append((da, db, c))
            for da, db, _ in passed:
                there = q_last.at[:, came_from(da, db)]
                send(there, there, fx_sems, (da, db), to_minor(db)).wait_recv()
            for c in copies + [c for _, _, c in passed]:
                c.wait_send()
            for k in range(units):
                coeffs_ref[:, k * wide : (k + 1) * wide] = from_slabs(q_last[k])
            continue

        part_sum = jnp.sum(square, axis=1, keepdims=True)
        l_own[...] = jnp.broadcast_to(part_sum, (8, LANES))
        here = q_all.at[me_s, :, me_c]
        copies = [send(here, here, a_sems, (d,), to_major(d)) for d in range(1, major)]
        l_copies = [send(l_own, l_client.at[d - 1], lc_sems, (d,), to_client(d)) for d in range(1, clients)]
        for c in copies + l_copies:
            c.start()
        sent = []

        def pass_on(da, db):
            n = da * minor + db
            here = q_all.at[me_s, :, came_from(da, db)]
            for dy in range(1, ys):
                sent.append(send(here, here, ay_sems, (n, dy), (me_c, 2 * lax.rem(me_y + dy, ys) + core)))
                sent[-1].start()
            sent.append(send(here, here, ac_sems, (n, 0), to_core))
            sent[-1].start()

        for da in range(major):
            if da > 0:
                copies[da - 1].wait_recv()
            here = q_all.at[me_s, :, came_from(da, 0)]
            for db in range(1, minor):
                sent.append(send(here, here, ax_sems, (da, db), to_minor(db)))
                sent[-1].start()
            pass_on(da, 0)
        for da in range(major):
            for db in range(1, minor):
                there = q_all.at[me_s, :, came_from(da, db)]
                send(there, there, ax_sems, (da, db), to_minor(db)).wait_recv()
                pass_on(da, db)
        for d, c in enumerate(l_copies, 1):
            c.wait()
            part_sum = part_sum + l_client[d - 1, 0:1, 0:1]
        l_part[...] = jnp.broadcast_to(part_sum, (8, LANES))
        l_copies = [send(l_part, l_shard.at[d - 1], ls_sems, (d,), to_shard(d)) for d in range(1, shards)]
        for c in l_copies:
            c.start()

        def multiply(owner):
            def body(k, _):
                at = pl.multiple_of(owner * span + k * wide, LANES)
                v = from_slabs(q_all[owner, k].astype(F32)).astype(BF16)
                acc[...] += nt(delta[:, pl.ds(at, wide)], v)
                return 0

            lax.fori_loop(0, units, body, 0)

        order = [(da, db) for db in range(minor) for da in range(major)]
        acc[...] = jnp.zeros_like(acc)
        multiply(me_s)
        for dy in range(1, ys):
            owner = 2 * lax.rem(me_y + ys - dy, ys) + core
            for da, db in order:
                n = da * minor + db
                there = q_all.at[owner, :, came_from(da, db)]
                send(there, there, ay_sems, (n, dy), to_core).wait_recv()
                sent.append(send(there, there, ac_sems, (n, dy), to_core))
                sent[-1].start()
        for dy in range(ys):
            owner = 2 * lax.rem(me_y + ys - dy, ys) + 1 - core
            for da, db in order:
                there = q_all.at[owner, :, came_from(da, db)]
                send(there, there, ac_sems, (da * minor + db, dy), to_core).wait_recv()
            multiply(owner)
            if dy > 0:
                continue
            for d in range(1, ys):
                multiply(2 * lax.rem(me_y + ys - d, ys) + core)
        for c in sent + copies:
            c.wait_send()
        for d, c in enumerate(l_copies, 1):
            c.wait()
            part_sum = part_sum + l_shard[d - 1, 0:1, 0:1]
        level = jnp.sqrt(part_sum / rank)


def on_device(clients, shards, delta, start_coeffs, noise_p, noise_q):
    rows, full = delta.shape[1:]
    rank = start_coeffs.shape[1]
    ys = shards // 2
    minor = 2
    major = clients // minor
    piece = rows // clients
    tiles = full // shards // LANES
    sub = next(
        s for s in range(1, tiles + 1)
        if tiles % s == 0 and (s * rank) % (8 * clients) == 0 and s * rank >= 32 * clients
    )
    units = tiles // sub
    unit = sub * rank // clients
    chunks = 7
    bounds = sorted({round(units * i / 3) for i in range(4)})
    groups = list(zip(bounds[:-1], bounds[1:]))
    parts = len(groups)
    panel_noise = noise_p.transpose(0, 2, 1)
    if piece % LANES:
        me = lax.axis_index("client")
        panel_noise = lax.dynamic_slice_in_dim(panel_noise, me * piece, piece, axis=2)

    dma = pltpu.SemaphoreType.DMA
    slab = (units, clients, unit, LANES)
    basis, coeffs = pl.pallas_call(
        functools.partial(kernel, (clients, shards, minor, sub, units, unit, chunks, groups)),
        out_shape=(
            jax.ShapeDtypeStruct((rank, rows), F32),
            jax.ShapeDtypeStruct((rank, full // shards), F32),
        ),
        in_specs=[pl.BlockSpec(memory_space=pl.ANY)] * 4,
        out_specs=[pl.BlockSpec(memory_space=pltpu.VMEM)] * 2,
        scratch_shapes=[
            pltpu.VMEM((rows, full), BF16),
            pltpu.VMEM((rank, full), BF16),
            pltpu.VMEM((ITERS, rank, piece), F32),
            pltpu.VMEM((rank, full // shards), F32),
            pltpu.VMEM(slab, F32),
            pltpu.VMEM((rows, rank), F32),
            pltpu.VMEM((8, LANES), F32),
            pltpu.VMEM((shards - 1, 8, LANES), F32),
            pltpu.VMEM((ITERS, clients, rank, piece), F32),
            pltpu.VMEM((ITERS, clients, rank, piece), F32),
            pltpu.VMEM((ITERS, clients, rank, piece), F32),
            pltpu.VMEM((ITERS, shards, rank, rank), F32),
            pltpu.VMEM((rank, rows), BF16),
            pltpu.VMEM((ITERS, ys) + slab, F32),
            pltpu.VMEM((ITERS, ys) + slab, F32),
            pltpu.VMEM(slab, F32),
            pltpu.VMEM((ITERS, ys - 1) + slab, BF16),
            pltpu.VMEM((ITERS, ys - 1) + slab, BF16),
            pltpu.VMEM((ITERS, clients, units, unit, LANES), BF16),
            pltpu.VMEM((ITERS, clients, units, unit, LANES), BF16),
            pltpu.VMEM((shards,) + slab, BF16),
            pltpu.VMEM(slab, F32),
            pltpu.VMEM((8, LANES), F32),
            pltpu.VMEM((clients - 1, 8, LANES), F32),
            pltpu.VMEM((8, LANES), F32),
            pltpu.VMEM((shards - 1, 8, LANES), F32),
            dma((chunks,)),
            dma((3,)),
            dma((shards - 1,)),
            dma((shards - 1,)),
            dma((2, ITERS, 2, clients)),
            dma((2, ITERS, shards)),
            dma((2, ITERS, ys, parts)),
            dma((2, ITERS, ys, parts)),
            dma((2, ITERS, clients, parts)),
            dma((2, major)),
            dma((2, major, minor)),
            dma((2, clients, ys)),
            dma((2, clients, ys)),
            dma((2, major)),
            dma((2, major, minor)),
            dma((2, clients)),
            dma((2, shards)),
        ],
        compiler_params=pltpu.CompilerParams(
            collective_id=0, has_side_effects=True, vmem_limit_bytes=60 * 1024 * 1024
        ),
        cost_estimate=pl.CostEstimate(
            flops=8 * rows * full * rank, bytes_accessed=2 * rows * full, transcendentals=0
        ),
    )(delta, start_coeffs.T, panel_noise, noise_q.transpose(0, 2, 1))
    return math.sqrt(rows * shards) * basis.T, coeffs.T + noise_q[ITERS - 1]


def solution(mesh):
    placed = (P("client", "shard", None), P(), P(None, "shard", None), P(None, "shard", None))
    return jax.shard_map(
        functools.partial(on_device, mesh.shape["client"], mesh.shape["shard"]),
        mesh=mesh,
        in_specs=placed,
        out_specs=(P("shard", None), P("shard", None)),
        check_vma=False,
    )
```

```python
import functools
import math

import jax
import jax.numpy as jnp
from jax import lax
from jax.experimental import pallas as pl
from jax.experimental.pallas import tpu as pltpu
from jax.sharding import PartitionSpec as P

ITERS = 2
EPS = 1e-06
CLIP_FRACTION = 0.5
LANES = 128
MESH = pl.DeviceIdType.MESH
F32 = jnp.float32
BF16 = jnp.bfloat16
HIGH = lax.Precision.HIGHEST


def nt(a, b, precision=None):
    return lax.dot_general(
        a, b, (((1,), (1,)), ((), ())), precision=precision, preferred_element_type=F32
    )


def inverse_lower(gram):
    n = gram.shape[0]
    tall = 8
    rows = lax.broadcasted_iota(jnp.int32, (n, n), 0)
    cols = lax.broadcasted_iota(jnp.int32, (n, n), 1)
    eye = (rows == cols).astype(F32)
    work = jnp.concatenate([gram, eye], axis=1)
    work = [work[i : i + tall] for i in range(0, n, tall)]
    at = lax.broadcasted_iota(jnp.int32, (tall, 2 * n), 0)
    many = 4
    done = []
    for j in range(0, n, many):
        b, r = j // tall, j % tall
        top = work[b]
        rows4 = [top[r + p : r + p + 1] for p in range(many)]
        head = [
            [jnp.broadcast_to(rows4[p][:, j + q : j + q + 1], (1, 2 * n)) if q >= p else None for q in range(many)]
            for p in range(many)
        ]
        inv = []
        for p in range(many):
            inv.append(1.0 / head[p][p])
            for q in range(p + 1, many):
                times = head[p][q] * inv[p]
                rows4[q] = rows4[q] - times * rows4[p]
                for t in range(q, many):
                    head[q][t] = head[q][t] - times * head[p][t]
        if r == 0:
            done.append(jnp.zeros((tall, 2 * n), F32))
        for p in range(many):
            done[-1] = jnp.where(at == r + p, rows4[p], done[-1])
        for i in range(b if r + many < tall else b + 1, n // tall):
            old = work[i]
            col = [jnp.broadcast_to(old[:, j + q : j + q + 1], (tall, 2 * n)) for q in range(many)]
            for p in range(many):
                times = col[p] * inv[p]
                old = old - times * rows4[p]
                for q in range(p + 1, many):
                    col[q] = col[q] - times * head[p][q]
            work[i] = old
    done = jnp.concatenate(done, axis=0)
    pivots = jnp.sum(done[:, :n] * eye, axis=1, keepdims=True)
    return done[:, n:] * (1.0 / jnp.sqrt(pivots))


def kernel(
    sizes, delta_hbm, start_hbm, noise_p_hbm, noise_q_hbm, basis_ref, coeffs_ref,
    delta, start, noise_p, noise_q, slabs, acc, sq_buf, sq_all, p_turned, p_send, p_recv, p_all, g_buf, pb,
    core_send, core_recv, own, y_send, y_recv, z_send, z_recv, q_all, q_last,
    l_own, l_client, l_part, l_shard,
    load_sem, extra_sem, small_send, small_recv, p_sems, pa_sems, px_sems, g_sems, core_sems, y_sems, z_sems,
    a_sems, ax_sems, ay_sems, ac_sems, f_sems, fx_sems, lc_sems, ls_sems,
):
    clients, shards, minor, sub, units, unit, chunks, groups = sizes
    major = clients // minor
    ys = shards // 2
    rows, full = delta.shape
    rank = start.shape[0]
    piece = rows // clients
    wide = sub * LANES
    span = units * wide
    me_c = lax.axis_index("client")
    me_s = lax.axis_index("shard")
    me_a, me_b = me_c // minor, lax.rem(me_c, minor)
    core = lax.rem(me_s, 2)
    me_y = me_s // 2
    chunk = full // chunks

    def load(i):
        return pltpu.make_async_copy(
            delta_hbm.at[0, :, pl.ds(i * chunk, chunk)],
            delta.at[:, pl.ds(i * chunk, chunk)],
            load_sem.at[i],
        )

    if piece % LANES == 0:
        mine_p = noise_p_hbm.at[:, :, pl.ds(pl.multiple_of(me_c * piece, LANES), piece)]
    else:
        mine_p = noise_p_hbm
    extras = [
        pltpu.make_async_copy(start_hbm, start, extra_sem.at[0]),
        pltpu.make_async_copy(mine_p, noise_p, extra_sem.at[1]),
        pltpu.make_async_copy(noise_q_hbm.at[0], noise_q, extra_sem.at[2]),
    ]
    extras[0].start()
    for i in range(chunks):
        load(i).start()
    extras[1].start()
    extras[2].start()

    barrier = pltpu.get_barrier_semaphore()
    for d in range(1, clients):
        pl.semaphore_signal(
            barrier, inc=1, device_id=(lax.rem(me_c + d, clients), me_s), device_id_type=MESH
        )
    for d in range(1, shards):
        pl.semaphore_signal(
            barrier, inc=1, device_id=(me_c, lax.rem(me_s + d, shards)), device_id_type=MESH
        )

    def send(src, dst, sems, index, device):
        return pltpu.make_async_remote_copy(
            src_ref=src, dst_ref=dst,
            send_sem=sems.at[(0,) + index], recv_sem=sems.at[(1,) + index],
            device_id=device, device_id_type=MESH,
        )

    def to_client(d):
        return (lax.rem(me_c + d, clients), me_s)

    def to_shard(d):
        return (me_c, lax.rem(me_s + d, shards))

    def to_major(d):
        return (lax.rem(me_a + d, major) * minor + me_b, me_s)

    def to_minor(d):
        return (me_a * minor + lax.rem(me_b + d, minor), me_s)

    def came_from(da, db):
        return lax.rem(me_a + major - da, major) * minor + lax.rem(me_b + minor - db, minor)

    to_core = (me_c, 2 * me_y + 1 - core)

    def to_slabs(v):
        v = jnp.concatenate([v[:, t * LANES : (t + 1) * LANES] for t in range(sub)], axis=0)
        return v.reshape(clients, unit, LANES)

    def from_slabs(v):
        v = v.reshape(sub * rank, LANES)
        return jnp.concatenate([v[t * rank : (t + 1) * rank] for t in range(sub)], axis=1)

    def begin(here, sems, key):
        copies = [send(here, here, sems, key + (d,), to_major(d)) for d in range(1, major)]
        for c in copies:
            c.start()
        return copies

    def finish(first, at, key, sems):
        passed = []
        for da in range(major):
            for g, copies in enumerate(first):
                if da > 0:
                    copies[da - 1].wait_recv()
                here = at(g, came_from(da, 0))
                for db in range(1, minor):
                    c = send(here, here, sems, key(g) + (da, db), to_minor(db))
                    c.start()
                    passed.append((g, da, db, c))
        for g, da, db, _ in passed:
            there = at(g, came_from(da, db))
            send(there, there, sems, key(g) + (da, db), to_minor(db)).wait_recv()
        for c in [c for copies in first for c in copies] + [p[3] for p in passed]:
            c.wait_send()

    extras[0].wait()

    def start_sum(i, total):
        v = start[:, pl.ds(pl.multiple_of(i * wide, LANES), wide)].astype(F32)
        return total + jnp.sum(v * v, axis=0, keepdims=True)

    level0 = jnp.sqrt(
        jnp.sum(lax.fori_loop(0, full // wide, start_sum, jnp.zeros((1, wide), F32)), axis=1, keepdims=True)
        / rank
    )

    acc[...] = jnp.zeros_like(acc)
    step = 512
    total = jnp.zeros((8, step), F32)
    for i in range(chunks):
        load(i).wait()

        def first(j, total, i=i):
            at = pl.multiple_of(i * chunk + j * step, step)
            acc[...] += nt(delta[:, pl.ds(at, step)], start[:, pl.ds(at, step)])

            for r in range(0, rows, 128):
                v = delta[r : r + 128, pl.ds(at, step)].astype(F32)
                total = total + jnp.sum((v * v).reshape(16, 8, step), axis=0)
            return total

        total = lax.fori_loop(0, chunk // step, first, total)

    pl.semaphore_wait(barrier, clients + shards - 2)

    mine = jnp.sum(jnp.sum(total, axis=0, keepdims=True), axis=1, keepdims=True)
    sq_buf[...] = jnp.broadcast_to(mine, (8, LANES))
    sq_copies = [
        pltpu.make_async_remote_copy(
            src_ref=sq_buf, dst_ref=sq_all.at[d - 1],
            send_sem=small_send.at[d - 1], recv_sem=small_recv.at[d - 1],
            device_id=to_shard(d), device_id_type=MESH,
        )
        for d in range(1, shards)
    ]
    for c in sq_copies:
        c.start()
    extras[1].wait()
    extras[2].wait()
    for k in range(units):
        slabs[k] = to_slabs(noise_q[:, k * wide : (k + 1) * wide])

    for it in range(ITERS):
        for d in range(clients):
            c = lax.rem(me_c + d, clients)
            v = acc[pl.ds(pl.multiple_of(c * piece, piece), piece), :]
            p_turned[d] = v.T
        if it == 0:
            level = level0
            sumsq = sq_buf[0:1, 0:1]
            for d, c in enumerate(sq_copies, 1):
                c.wait()
                sumsq = sumsq + sq_all[d - 1, 0:1, 0:1]
            count = rows * shards * full
            factor = jnp.minimum(1.0, CLIP_FRACTION * math.sqrt(count) / jnp.sqrt(sumsq + EPS))
        copies = [
            send(p_send.at[it, d], p_recv.at[it, d], p_sems, (it, d), to_client(d))
            for d in range(1, clients)
        ]
        for d, c in enumerate(copies, 1):
            p_send[it, d] = (p_turned[d] * factor).astype(BF16)
            c.start()
        v = p_turned[0] * factor + level * noise_p[it]
        for d, c in enumerate(copies, 1):
            c.wait()
            v = v + p_recv[it, d].astype(F32)
        p_all[it, me_c] = v
        copies = begin(p_all.at[it, me_c], pa_sems, (it,))
        finish([copies], lambda g, who, it=it: p_all.at[it, who], lambda g, it=it: (it,), px_sems)

        panel = jnp.concatenate([p_all[it, c] for c in range(clients)], axis=1)
        gram = nt(panel, panel, HIGH)
        g_buf[it, 0] = gram
        copies = [
            send(g_buf.at[it, 0], g_buf.at[it, d], g_sems, (it, d), to_shard(d))
            for d in range(1, shards)
        ]
        for c in copies:
            c.start()
        for d, c in enumerate(copies, 1):
            c.wait()
            gram = gram + g_buf[it, d]
        panel = jnp.dot(inverse_lower(gram), panel, precision=HIGH, preferred_element_type=F32)
        pb[...] = panel.astype(BF16)
        if it == ITERS - 1:
            basis_ref[...] = panel

        def block(owner, k):
            at = pl.multiple_of(owner * span + k * wide, LANES)
            return to_slabs(factor * jnp.dot(pb[...], delta[:, pl.ds(at, wide)], preferred_element_type=F32))

        y_copies = []
        for dy in list(range(1, ys)) + [0]:
            to_y = lax.rem(me_y + dy, ys)
            core_copies = []

            def run_other(g, to_y=to_y, dy=dy):
                k0, k1 = groups[g]

                def other(k, _):
                    core_send[it, dy, k] = block(2 * to_y + 1 - core, k)
                    return 0

                lax.fori_loop(k0, k1, other, 0)
                part = pl.ds(k0, k1 - k0)
                c = send(core_send.at[it, dy, part], core_recv.at[it, dy, part], core_sems, (it, dy, g), to_core)
                c.start()
                core_copies.append(c)

            def run_same(g, to_y=to_y, dy=dy):
                k0, k1 = groups[g]

                def same(k, _):
                    own[k] = block(2 * to_y + core, k)
                    return 0

                def add_core(k, _):
                    v = own[k] + core_recv[it, dy, k]
                    if dy > 0:
                        y_send[it, dy - 1, k] = v.astype(BF16)
                    else:
                        own[k] = v
                    return 0

                lax.fori_loop(k0, k1, same, 0)
                core_copies[g].wait()
                lax.fori_loop(k0, k1, add_core, 0)
                if dy > 0:
                    part = pl.ds(k0, k1 - k0)
                    c = send(
                        y_send.at[it, dy - 1, part], y_recv.at[it, dy - 1, part],
                        y_sems, (it, dy, g), (me_c, 2 * to_y + core),
                    )
                    c.start()
                    y_copies.append((g, c))

            run_other(0)
            for g in range(len(groups)):
                if g + 1 < len(groups):
                    run_other(g + 1)
                run_same(g)
        z_copies = []
        for g, (k0, k1) in enumerate(groups):
            for h, c in y_copies:
                if h == g:
                    c.wait()

            def add_y(k, _):
                v = own[k]
                for d in range(1, ys):
                    v = v + y_recv[it, d - 1, k].astype(F32)
                own[k] = v
                for c in range(clients):
                    z_send[it, c, k] = v[c].astype(BF16)
                return 0

            lax.fori_loop(k0, k1, add_y, 0)
            part = pl.ds(k0, k1 - k0)
            for d in range(1, clients):
                c = send(
                    z_send.at[it, lax.rem(me_c + d, clients), part], z_recv.at[it, d, part],
                    z_sems, (it, d, g), to_client(d),
                )
                c.start()
                z_copies.append((g, c))

        square = jnp.zeros((1, LANES), F32)
        last = []
        for g, (k0, k1) in enumerate(groups):
            for h, c in z_copies:
                if h == g:
                    c.wait()
            for k in range(k0, k1):
                v = own[k, me_c]
                for d in range(1, clients):
                    v = v + z_recv[it, d, k].astype(F32)
                if it < ITERS - 1:
                    v = v + slabs[k, me_c]
                    square = square + jnp.sum(v * v, axis=0, keepdims=True)
                    q_all[me_s, k, me_c] = v.astype(BF16)
                else:
                    q_last[k, me_c] = v
            if it == ITERS - 1:
                last.append(begin(q_last.at[pl.ds(k0, k1 - k0), me_c], f_sems, (g,)))

        if it == ITERS - 1:
            finish(
                last,
                lambda g, who: q_last.at[pl.ds(groups[g][0], groups[g][1] - groups[g][0]), who],
                lambda g: (g,),
                fx_sems,
            )
            for k in range(units):
                coeffs_ref[:, k * wide : (k + 1) * wide] = from_slabs(q_last[k])
            continue

        part_sum = jnp.sum(square, axis=1, keepdims=True)
        l_own[...] = jnp.broadcast_to(part_sum, (8, LANES))
        here = q_all.at[me_s, :, me_c]
        copies = [send(here, here, a_sems, (d,), to_major(d)) for d in range(1, major)]
        l_copies = [send(l_own, l_client.at[d - 1], lc_sems, (d,), to_client(d)) for d in range(1, clients)]
        for c in copies + l_copies:
            c.start()
        sent = []

        def pass_on(da, db):
            n = da * minor + db
            here = q_all.at[me_s, :, came_from(da, db)]
            for dy in range(1, ys):
                sent.append(send(here, here, ay_sems, (n, dy), (me_c, 2 * lax.rem(me_y + dy, ys) + core)))
                sent[-1].start()
            sent.append(send(here, here, ac_sems, (n, 0), to_core))
            sent[-1].start()

        for da in range(major):
            if da > 0:
                copies[da - 1].wait_recv()
            here = q_all.at[me_s, :, came_from(da, 0)]
            for db in range(1, minor):
                sent.append(send(here, here, ax_sems, (da, db), to_minor(db)))
                sent[-1].start()
            pass_on(da, 0)
        for da in range(major):
            for db in range(1, minor):
                there = q_all.at[me_s, :, came_from(da, db)]
                send(there, there, ax_sems, (da, db), to_minor(db)).wait_recv()
                pass_on(da, db)
        for d, c in enumerate(l_copies, 1):
            c.wait()
            part_sum = part_sum + l_client[d - 1, 0:1, 0:1]
        l_part[...] = jnp.broadcast_to(part_sum, (8, LANES))
        l_copies = [send(l_part, l_shard.at[d - 1], ls_sems, (d,), to_shard(d)) for d in range(1, shards)]
        for c in l_copies:
            c.start()

        def multiply(owner):
            def body(k, _):
                at = pl.multiple_of(owner * span + k * wide, LANES)
                v = from_slabs(q_all[owner, k].astype(F32)).astype(BF16)
                acc[...] += nt(delta[:, pl.ds(at, wide)], v)
                return 0

            lax.fori_loop(0, units, body, 0)

        order = [(da, db) for db in range(minor) for da in range(major)]
        acc[...] = jnp.zeros_like(acc)
        multiply(me_s)
        for dy in range(1, ys):
            owner = 2 * lax.rem(me_y + ys - dy, ys) + core
            for da, db in order:
                n = da * minor + db
                there = q_all.at[owner, :, came_from(da, db)]
                send(there, there, ay_sems, (n, dy), to_core).wait_recv()
                sent.append(send(there, there, ac_sems, (n, dy), to_core))
                sent[-1].start()
        for dy in range(ys):
            owner = 2 * lax.rem(me_y + ys - dy, ys) + 1 - core
            for da, db in order:
                there = q_all.at[owner, :, came_from(da, db)]
                send(there, there, ac_sems, (da * minor + db, dy), to_core).wait_recv()
            multiply(owner)
            if dy > 0:
                continue
            for d in range(1, ys):
                multiply(2 * lax.rem(me_y + ys - d, ys) + core)
        for c in sent + copies:
            c.wait_send()
        for d, c in enumerate(l_copies, 1):
            c.wait()
            part_sum = part_sum + l_shard[d - 1, 0:1, 0:1]
        level = jnp.sqrt(part_sum / rank)


def on_device(clients, shards, delta, start_coeffs, noise_p, noise_q):
    rows, full = delta.shape[1:]
    rank = start_coeffs.shape[1]
    ys = shards // 2
    minor = 2
    major = clients // minor
    piece = rows // clients
    tiles = full // shards // LANES
    sub = next(
        s for s in range(1, tiles + 1)
        if tiles % s == 0 and (s * rank) % (8 * clients) == 0 and s * rank >= 32 * clients
    )
    units = tiles // sub
    unit = sub * rank // clients
    chunks = 7
    bounds = sorted({round(units * i / 3) for i in range(4)})
    groups = list(zip(bounds[:-1], bounds[1:]))
    parts = len(groups)
    panel_noise = noise_p.transpose(0, 2, 1)
    if piece % LANES:
        me = lax.axis_index("client")
        panel_noise = lax.dynamic_slice_in_dim(panel_noise, me * piece, piece, axis=2)

    dma = pltpu.SemaphoreType.DMA
    slab = (units, clients, unit, LANES)
    basis, coeffs = pl.pallas_call(
        functools.partial(kernel, (clients, shards, minor, sub, units, unit, chunks, groups)),
        out_shape=(
            jax.ShapeDtypeStruct((rank, rows), F32),
            jax.ShapeDtypeStruct((rank, full // shards), F32),
        ),
        in_specs=[pl.BlockSpec(memory_space=pl.ANY)] * 4,
        out_specs=[pl.BlockSpec(memory_space=pltpu.VMEM)] * 2,
        scratch_shapes=[
            pltpu.VMEM((rows, full), BF16),
            pltpu.VMEM((rank, full), BF16),
            pltpu.VMEM((ITERS, rank, piece), F32),
            pltpu.VMEM((rank, full // shards), F32),
            pltpu.VMEM(slab, F32),
            pltpu.VMEM((rows, rank), F32),
            pltpu.VMEM((8, LANES), F32),
            pltpu.VMEM((shards - 1, 8, LANES), F32),
            pltpu.VMEM((clients, rank, piece), F32),
            pltpu.VMEM((ITERS, clients, rank, piece), BF16),
            pltpu.VMEM((ITERS, clients, rank, piece), BF16),
            pltpu.VMEM((ITERS, clients, rank, piece), F32),
            pltpu.VMEM((ITERS, shards, rank, rank), F32),
            pltpu.VMEM((rank, rows), BF16),
            pltpu.VMEM((ITERS, ys) + slab, F32),
            pltpu.VMEM((ITERS, ys) + slab, F32),
            pltpu.VMEM(slab, F32),
            pltpu.VMEM((ITERS, ys - 1) + slab, BF16),
            pltpu.VMEM((ITERS, ys - 1) + slab, BF16),
            pltpu.VMEM((ITERS, clients, units, unit, LANES), BF16),
            pltpu.VMEM((ITERS, clients, units, unit, LANES), BF16),
            pltpu.VMEM((shards,) + slab, BF16),
            pltpu.VMEM(slab, F32),
            pltpu.VMEM((8, LANES), F32),
            pltpu.VMEM((clients - 1, 8, LANES), F32),
            pltpu.VMEM((8, LANES), F32),
            pltpu.VMEM((shards - 1, 8, LANES), F32),
            dma((chunks,)),
            dma((3,)),
            dma((shards - 1,)),
            dma((shards - 1,)),
            dma((2, ITERS, clients)),
            dma((2, ITERS, major)),
            dma((2, ITERS, major, minor)),
            dma((2, ITERS, shards)),
            dma((2, ITERS, ys, parts)),
            dma((2, ITERS, ys, parts)),
            dma((2, ITERS, clients, parts)),
            dma((2, major)),
            dma((2, major, minor)),
            dma((2, clients, ys)),
            dma((2, clients, ys)),
            dma((2, parts, major)),
            dma((2, parts, major, minor)),
            dma((2, clients)),
            dma((2, shards)),
        ],
        compiler_params=pltpu.CompilerParams(
            collective_id=0, has_side_effects=True, vmem_limit_bytes=60 * 1024 * 1024
        ),
        cost_estimate=pl.CostEstimate(
            flops=8 * rows * full * rank, bytes_accessed=2 * rows * full, transcendentals=0
        ),
    )(delta, start_coeffs.T, panel_noise, noise_q.transpose(0, 2, 1))
    return math.sqrt(rows * shards) * basis.T, coeffs.T + noise_q[ITERS - 1]


def solution(mesh):
    placed = (P("client", "shard", None), P(), P(None, "shard", None), P(None, "shard", None))
    return jax.shard_map(
        functools.partial(on_device, mesh.shape["client"], mesh.shape["shard"]),
        mesh=mesh,
        in_specs=placed,
        out_specs=(P("shard", None), P("shard", None)),
        check_vma=False,
    )
```

```python
import functools
import math

import jax
import jax.numpy as jnp
from jax import lax
from jax.experimental import pallas as pl
from jax.experimental.pallas import tpu as pltpu
from jax.sharding import PartitionSpec as P

ITERS = 2
EPS = 1e-06
CLIP_FRACTION = 0.5
LANES = 128
MESH = pl.DeviceIdType.MESH
F32 = jnp.float32
BF16 = jnp.bfloat16
HIGH = lax.Precision.HIGHEST


def nt(a, b, precision=None):
    return lax.dot_general(
        a, b, (((1,), (1,)), ((), ())), precision=precision, preferred_element_type=F32
    )


def inverse_lower(gram):
    n = gram.shape[0]
    tall = 8
    rows = lax.broadcasted_iota(jnp.int32, (n, n), 0)
    cols = lax.broadcasted_iota(jnp.int32, (n, n), 1)
    eye = (rows == cols).astype(F32)
    work = jnp.concatenate([gram, eye], axis=1)
    work = [work[i : i + tall] for i in range(0, n, tall)]
    at = lax.broadcasted_iota(jnp.int32, (tall, 2 * n), 0)
    many = 4
    done = []
    for j in range(0, n, many):
        b, r = j // tall, j % tall
        top = work[b]
        rows4 = [top[r + p : r + p + 1] for p in range(many)]
        head = [
            [jnp.broadcast_to(rows4[p][:, j + q : j + q + 1], (1, 2 * n)) if q >= p else None for q in range(many)]
            for p in range(many)
        ]
        inv = []
        for p in range(many):
            inv.append(1.0 / head[p][p])
            for q in range(p + 1, many):
                times = head[p][q] * inv[p]
                rows4[q] = rows4[q] - times * rows4[p]
                for t in range(q, many):
                    head[q][t] = head[q][t] - times * head[p][t]
        if r == 0:
            done.append(jnp.zeros((tall, 2 * n), F32))
        for p in range(many):
            done[-1] = jnp.where(at == r + p, rows4[p], done[-1])
        for i in range(b if r + many < tall else b + 1, n // tall):
            old = work[i]
            col = [jnp.broadcast_to(old[:, j + q : j + q + 1], (tall, 2 * n)) for q in range(many)]
            for p in range(many):
                times = col[p] * inv[p]
                old = old - times * rows4[p]
                for q in range(p + 1, many):
                    col[q] = col[q] - times * head[p][q]
            work[i] = old
    done = jnp.concatenate(done, axis=0)
    pivots = jnp.sum(done[:, :n] * eye, axis=1, keepdims=True)
    return done[:, n:] * (1.0 / jnp.sqrt(pivots))


def kernel(
    sizes, delta_hbm, start_hbm, noise_p_hbm, noise_q_hbm, basis_ref, coeffs_ref,
    delta, start, noise_p, noise_q, slabs, acc, sq_buf, sq_all, p_turned, p_send, p_recv, p_send_last, p_recv_last, p_all, g_buf, pb,
    core_send, core_recv, own, y_send, y_recv, z_send, z_recv, q_all, q_last,
    l_own, l_client, l_part, l_shard,
    load_sem, extra_sem, small_send, small_recv, p_sems, pa_sems, px_sems, g_sems, core_sems, y_sems, z_sems,
    a_sems, ax_sems, ay_sems, ac_sems, f_sems, fx_sems, lc_sems, ls_sems,
):
    clients, shards, minor, sub, units, unit, chunks, groups = sizes
    major = clients // minor
    ys = shards // 2
    rows, full = delta.shape
    rank = start.shape[0]
    piece = rows // clients
    wide = sub * LANES
    span = units * wide
    me_c = lax.axis_index("client")
    me_s = lax.axis_index("shard")
    me_a, me_b = me_c // minor, lax.rem(me_c, minor)
    core = lax.rem(me_s, 2)
    me_y = me_s // 2
    chunk = full // chunks

    def load(i):
        return pltpu.make_async_copy(
            delta_hbm.at[0, :, pl.ds(i * chunk, chunk)],
            delta.at[:, pl.ds(i * chunk, chunk)],
            load_sem.at[i],
        )

    if piece % LANES == 0:
        mine_p = noise_p_hbm.at[:, :, pl.ds(pl.multiple_of(me_c * piece, LANES), piece)]
    else:
        mine_p = noise_p_hbm
    extras = [
        pltpu.make_async_copy(start_hbm, start, extra_sem.at[0]),
        pltpu.make_async_copy(mine_p, noise_p, extra_sem.at[1]),
        pltpu.make_async_copy(noise_q_hbm.at[0], noise_q, extra_sem.at[2]),
    ]
    extras[0].start()
    for i in range(chunks):
        load(i).start()
    extras[1].start()
    extras[2].start()

    barrier = pltpu.get_barrier_semaphore()
    for d in range(1, clients):
        pl.semaphore_signal(
            barrier, inc=1, device_id=(lax.rem(me_c + d, clients), me_s), device_id_type=MESH
        )
    for d in range(1, shards):
        pl.semaphore_signal(
            barrier, inc=1, device_id=(me_c, lax.rem(me_s + d, shards)), device_id_type=MESH
        )

    def send(src, dst, sems, index, device):
        return pltpu.make_async_remote_copy(
            src_ref=src, dst_ref=dst,
            send_sem=sems.at[(0,) + index], recv_sem=sems.at[(1,) + index],
            device_id=device, device_id_type=MESH,
        )

    def to_client(d):
        return (lax.rem(me_c + d, clients), me_s)

    def to_shard(d):
        return (me_c, lax.rem(me_s + d, shards))

    def to_major(d):
        return (lax.rem(me_a + d, major) * minor + me_b, me_s)

    def to_minor(d):
        return (me_a * minor + lax.rem(me_b + d, minor), me_s)

    def came_from(da, db):
        return lax.rem(me_a + major - da, major) * minor + lax.rem(me_b + minor - db, minor)

    to_core = (me_c, 2 * me_y + 1 - core)

    def to_slabs(v):
        v = jnp.concatenate([v[:, t * LANES : (t + 1) * LANES] for t in range(sub)], axis=0)
        return v.reshape(clients, unit, LANES)

    def from_slabs(v):
        v = v.reshape(sub * rank, LANES)
        return jnp.concatenate([v[t * rank : (t + 1) * rank] for t in range(sub)], axis=1)

    def begin(here, sems, key):
        copies = [send(here, here, sems, key + (d,), to_major(d)) for d in range(1, major)]
        for c in copies:
            c.start()
        return copies

    def finish(first, at, key, sems):
        passed = []
        for da in range(major):
            for g, copies in enumerate(first):
                if da > 0:
                    copies[da - 1].wait_recv()
                here = at(g, came_from(da, 0))
                for db in range(1, minor):
                    c = send(here, here, sems, key(g) + (da, db), to_minor(db))
                    c.start()
                    passed.append((g, da, db, c))
        for g, da, db, _ in passed:
            there = at(g, came_from(da, db))
            send(there, there, sems, key(g) + (da, db), to_minor(db)).wait_recv()
        for c in [c for copies in first for c in copies] + [p[3] for p in passed]:
            c.wait_send()

    extras[0].wait()

    def start_sum(i, total):
        v = start[:, pl.ds(pl.multiple_of(i * wide, LANES), wide)].astype(F32)
        return total + jnp.sum(v * v, axis=0, keepdims=True)

    level0 = jnp.sqrt(
        jnp.sum(lax.fori_loop(0, full // wide, start_sum, jnp.zeros((1, wide), F32)), axis=1, keepdims=True)
        / rank
    )

    acc[...] = jnp.zeros_like(acc)
    step = 512
    total = jnp.zeros((8, step), F32)
    for i in range(chunks):
        load(i).wait()

        def first(j, total, i=i):
            at = pl.multiple_of(i * chunk + j * step, step)
            acc[...] += nt(delta[:, pl.ds(at, step)], start[:, pl.ds(at, step)])

            for r in range(0, rows, 128):
                v = delta[r : r + 128, pl.ds(at, step)].astype(F32)
                total = total + jnp.sum((v * v).reshape(16, 8, step), axis=0)
            return total

        total = lax.fori_loop(0, chunk // step, first, total)

    pl.semaphore_wait(barrier, clients + shards - 2)

    mine = jnp.sum(jnp.sum(total, axis=0, keepdims=True), axis=1, keepdims=True)
    sq_buf[...] = jnp.broadcast_to(mine, (8, LANES))
    sq_copies = [
        pltpu.make_async_remote_copy(
            src_ref=sq_buf, dst_ref=sq_all.at[d - 1],
            send_sem=small_send.at[d - 1], recv_sem=small_recv.at[d - 1],
            device_id=to_shard(d), device_id_type=MESH,
        )
        for d in range(1, shards)
    ]
    for c in sq_copies:
        c.start()
    extras[1].wait()
    extras[2].wait()
    for k in range(units):
        slabs[k] = to_slabs(noise_q[:, k * wide : (k + 1) * wide])

    for it in range(ITERS):
        p_out, p_in = (p_send_last, p_recv_last) if it == ITERS - 1 else (p_send.at[it], p_recv.at[it])
        for d in range(clients):
            c = lax.rem(me_c + d, clients)
            v = acc[pl.ds(pl.multiple_of(c * piece, piece), piece), :]
            p_turned[d] = v.T
        if it == 0:
            level = level0
            sumsq = sq_buf[0:1, 0:1]
            for d, c in enumerate(sq_copies, 1):
                c.wait()
                sumsq = sumsq + sq_all[d - 1, 0:1, 0:1]
            count = rows * shards * full
            factor = jnp.minimum(1.0, CLIP_FRACTION * math.sqrt(count) / jnp.sqrt(sumsq + EPS))
        copies = [
            send(p_out.at[d], p_in.at[d], p_sems, (it, d), to_client(d))
            for d in range(1, clients)
        ]
        for d, c in enumerate(copies, 1):
            p_out[d] = (p_turned[d] * factor).astype(p_out.dtype)
            c.start()
        v = p_turned[0] * factor + level * noise_p[it]
        for d, c in enumerate(copies, 1):
            c.wait()
            v = v + p_in[d].astype(F32)
        p_all[it, me_c] = v
        copies = begin(p_all.at[it, me_c], pa_sems, (it,))
        finish([copies], lambda g, who, it=it: p_all.at[it, who], lambda g, it=it: (it,), px_sems)

        panel = jnp.concatenate([p_all[it, c] for c in range(clients)], axis=1)
        gram = nt(panel, panel, HIGH)
        g_buf[it, 0] = gram
        copies = [
            send(g_buf.at[it, 0], g_buf.at[it, d], g_sems, (it, d), to_shard(d))
            for d in range(1, shards)
        ]
        for c in copies:
            c.start()
        for d, c in enumerate(copies, 1):
            c.wait()
            gram = gram + g_buf[it, d]
        panel = jnp.dot(inverse_lower(gram), panel, precision=HIGH, preferred_element_type=F32)
        pb[...] = panel.astype(BF16)
        if it == ITERS - 1:
            basis_ref[...] = panel

        def block(owner, k):
            at = pl.multiple_of(owner * span + k * wide, LANES)
            return to_slabs(factor * jnp.dot(pb[...], delta[:, pl.ds(at, wide)], preferred_element_type=F32))

        y_copies = []
        for dy in list(range(1, ys)) + [0]:
            to_y = lax.rem(me_y + dy, ys)
            core_copies = []

            def run_other(g, to_y=to_y, dy=dy):
                k0, k1 = groups[g]

                def other(k, _):
                    core_send[it, dy, k] = block(2 * to_y + 1 - core, k)
                    return 0

                lax.fori_loop(k0, k1, other, 0)
                part = pl.ds(k0, k1 - k0)
                c = send(core_send.at[it, dy, part], core_recv.at[it, dy, part], core_sems, (it, dy, g), to_core)
                c.start()
                core_copies.append(c)

            def run_same(g, to_y=to_y, dy=dy):
                k0, k1 = groups[g]

                def same(k, _):
                    own[k] = block(2 * to_y + core, k)
                    return 0

                def add_core(k, _):
                    v = own[k] + core_recv[it, dy, k]
                    if dy > 0:
                        y_send[it, dy - 1, k] = v.astype(BF16)
                    else:
                        own[k] = v
                    return 0

                lax.fori_loop(k0, k1, same, 0)
                core_copies[g].wait()
                lax.fori_loop(k0, k1, add_core, 0)
                if dy > 0:
                    part = pl.ds(k0, k1 - k0)
                    c = send(
                        y_send.at[it, dy - 1, part], y_recv.at[it, dy - 1, part],
                        y_sems, (it, dy, g), (me_c, 2 * to_y + core),
                    )
                    c.start()
                    y_copies.append((g, c))

            run_other(0)
            for g in range(len(groups)):
                if g + 1 < len(groups):
                    run_other(g + 1)
                run_same(g)
        z_copies = []
        for g, (k0, k1) in enumerate(groups):
            for h, c in y_copies:
                if h == g:
                    c.wait()

            def add_y(k, _):
                v = own[k]
                for d in range(1, ys):
                    v = v + y_recv[it, d - 1, k].astype(F32)
                own[k] = v
                for c in range(clients):
                    z_send[it, c, k] = v[c].astype(BF16)
                return 0

            lax.fori_loop(k0, k1, add_y, 0)
            part = pl.ds(k0, k1 - k0)
            for d in range(1, clients):
                c = send(
                    z_send.at[it, lax.rem(me_c + d, clients), part], z_recv.at[it, d, part],
                    z_sems, (it, d, g), to_client(d),
                )
                c.start()
                z_copies.append((g, c))

        square = jnp.zeros((1, LANES), F32)
        last = []
        for g, (k0, k1) in enumerate(groups):
            for h, c in z_copies:
                if h == g:
                    c.wait()
            for k in range(k0, k1):
                v = own[k, me_c]
                for d in range(1, clients):
                    v = v + z_recv[it, d, k].astype(F32)
                if it < ITERS - 1:
                    v = v + slabs[k, me_c]
                    square = square + jnp.sum(v * v, axis=0, keepdims=True)
                    q_all[me_s, k, me_c] = v.astype(BF16)
                else:
                    q_last[k, me_c] = v
            if it == ITERS - 1:
                last.append(begin(q_last.at[pl.ds(k0, k1 - k0), me_c], f_sems, (g,)))

        if it == ITERS - 1:
            finish(
                last,
                lambda g, who: q_last.at[pl.ds(groups[g][0], groups[g][1] - groups[g][0]), who],
                lambda g: (g,),
                fx_sems,
            )
            for k in range(units):
                coeffs_ref[:, k * wide : (k + 1) * wide] = from_slabs(q_last[k])
            continue

        part_sum = jnp.sum(square, axis=1, keepdims=True)
        l_own[...] = jnp.broadcast_to(part_sum, (8, LANES))
        here = q_all.at[me_s, :, me_c]
        copies = [send(here, here, a_sems, (d,), to_major(d)) for d in range(1, major)]
        l_copies = [send(l_own, l_client.at[d - 1], lc_sems, (d,), to_client(d)) for d in range(1, clients)]
        for c in copies + l_copies:
            c.start()
        sent = []

        def pass_on(da, db):
            n = da * minor + db
            here = q_all.at[me_s, :, came_from(da, db)]
            for dy in range(1, ys):
                sent.append(send(here, here, ay_sems, (n, dy), (me_c, 2 * lax.rem(me_y + dy, ys) + core)))
                sent[-1].start()
            sent.append(send(here, here, ac_sems, (n, 0), to_core))
            sent[-1].start()

        for da in range(major):
            if da > 0:
                copies[da - 1].wait_recv()
            here = q_all.at[me_s, :, came_from(da, 0)]
            for db in range(1, minor):
                sent.append(send(here, here, ax_sems, (da, db), to_minor(db)))
                sent[-1].start()
            pass_on(da, 0)
        for da in range(major):
            for db in range(1, minor):
                there = q_all.at[me_s, :, came_from(da, db)]
                send(there, there, ax_sems, (da, db), to_minor(db)).wait_recv()
                pass_on(da, db)
        for d, c in enumerate(l_copies, 1):
            c.wait()
            part_sum = part_sum + l_client[d - 1, 0:1, 0:1]
        l_part[...] = jnp.broadcast_to(part_sum, (8, LANES))
        l_copies = [send(l_part, l_shard.at[d - 1], ls_sems, (d,), to_shard(d)) for d in range(1, shards)]
        for c in l_copies:
            c.start()

        def multiply(owner):
            def body(k, _):
                at = pl.multiple_of(owner * span + k * wide, LANES)
                v = from_slabs(q_all[owner, k].astype(F32)).astype(BF16)
                acc[...] += nt(delta[:, pl.ds(at, wide)], v)
                return 0

            lax.fori_loop(0, units, body, 0)

        order = [(da, db) for db in range(minor) for da in range(major)]
        acc[...] = jnp.zeros_like(acc)
        multiply(me_s)
        for dy in range(1, ys):
            owner = 2 * lax.rem(me_y + ys - dy, ys) + core
            for da, db in order:
                n = da * minor + db
                there = q_all.at[owner, :, came_from(da, db)]
                send(there, there, ay_sems, (n, dy), to_core).wait_recv()
                sent.append(send(there, there, ac_sems, (n, dy), to_core))
                sent[-1].start()
        for dy in range(ys):
            owner = 2 * lax.rem(me_y + ys - dy, ys) + 1 - core
            for da, db in order:
                there = q_all.at[owner, :, came_from(da, db)]
                send(there, there, ac_sems, (da * minor + db, dy), to_core).wait_recv()
            multiply(owner)
            if dy > 0:
                continue
            for d in range(1, ys):
                multiply(2 * lax.rem(me_y + ys - d, ys) + core)
        for c in sent + copies:
            c.wait_send()
        for d, c in enumerate(l_copies, 1):
            c.wait()
            part_sum = part_sum + l_shard[d - 1, 0:1, 0:1]
        level = jnp.sqrt(part_sum / rank)


def on_device(clients, shards, delta, start_coeffs, noise_p, noise_q):
    rows, full = delta.shape[1:]
    rank = start_coeffs.shape[1]
    ys = shards // 2
    minor = 2
    major = clients // minor
    piece = rows // clients
    tiles = full // shards // LANES
    sub = next(
        s for s in range(1, tiles + 1)
        if tiles % s == 0 and (s * rank) % (8 * clients) == 0 and s * rank >= 32 * clients
    )
    units = tiles // sub
    unit = sub * rank // clients
    chunks = 7
    bounds = sorted({round(units * i / 3) for i in range(4)})
    groups = list(zip(bounds[:-1], bounds[1:]))
    parts = len(groups)
    panel_noise = noise_p.transpose(0, 2, 1)
    if piece % LANES:
        me = lax.axis_index("client")
        panel_noise = lax.dynamic_slice_in_dim(panel_noise, me * piece, piece, axis=2)

    dma = pltpu.SemaphoreType.DMA
    slab = (units, clients, unit, LANES)
    basis, coeffs = pl.pallas_call(
        functools.partial(kernel, (clients, shards, minor, sub, units, unit, chunks, groups)),
        out_shape=(
            jax.ShapeDtypeStruct((rank, rows), F32),
            jax.ShapeDtypeStruct((rank, full // shards), F32),
        ),
        in_specs=[pl.BlockSpec(memory_space=pl.ANY)] * 4,
        out_specs=[pl.BlockSpec(memory_space=pltpu.VMEM)] * 2,
        scratch_shapes=[
            pltpu.VMEM((rows, full), BF16),
            pltpu.VMEM((rank, full), BF16),
            pltpu.VMEM((ITERS, rank, piece), F32),
            pltpu.VMEM((rank, full // shards), F32),
            pltpu.VMEM(slab, F32),
            pltpu.VMEM((rows, rank), F32),
            pltpu.VMEM((8, LANES), F32),
            pltpu.VMEM((shards - 1, 8, LANES), F32),
            pltpu.VMEM((clients, rank, piece), F32),
            pltpu.VMEM((ITERS - 1, clients, rank, piece), BF16),
            pltpu.VMEM((ITERS - 1, clients, rank, piece), BF16),
            pltpu.VMEM((clients, rank, piece), F32),
            pltpu.VMEM((clients, rank, piece), F32),
            pltpu.VMEM((ITERS, clients, rank, piece), F32),
            pltpu.VMEM((ITERS, shards, rank, rank), F32),
            pltpu.VMEM((rank, rows), BF16),
            pltpu.VMEM((ITERS, ys) + slab, F32),
            pltpu.VMEM((ITERS, ys) + slab, F32),
            pltpu.VMEM(slab, F32),
            pltpu.VMEM((ITERS, ys - 1) + slab, BF16),
            pltpu.VMEM((ITERS, ys - 1) + slab, BF16),
            pltpu.VMEM((ITERS, clients, units, unit, LANES), BF16),
            pltpu.VMEM((ITERS, clients, units, unit, LANES), BF16),
            pltpu.VMEM((shards,) + slab, BF16),
            pltpu.VMEM(slab, F32),
            pltpu.VMEM((8, LANES), F32),
            pltpu.VMEM((clients - 1, 8, LANES), F32),
            pltpu.VMEM((8, LANES), F32),
            pltpu.VMEM((shards - 1, 8, LANES), F32),
            dma((chunks,)),
            dma((3,)),
            dma((shards - 1,)),
            dma((shards - 1,)),
            dma((2, ITERS, clients)),
            dma((2, ITERS, major)),
            dma((2, ITERS, major, minor)),
            dma((2, ITERS, shards)),
            dma((2, ITERS, ys, parts)),
            dma((2, ITERS, ys, parts)),
            dma((2, ITERS, clients, parts)),
            dma((2, major)),
            dma((2, major, minor)),
            dma((2, clients, ys)),
            dma((2, clients, ys)),
            dma((2, parts, major)),
            dma((2, parts, major, minor)),
            dma((2, clients)),
            dma((2, shards)),
        ],
        compiler_params=pltpu.CompilerParams(
            collective_id=0, has_side_effects=True, vmem_limit_bytes=60 * 1024 * 1024
        ),
        cost_estimate=pl.CostEstimate(
            flops=8 * rows * full * rank, bytes_accessed=2 * rows * full, transcendentals=0
        ),
    )(delta, start_coeffs.T, panel_noise, noise_q.transpose(0, 2, 1))
    return math.sqrt(rows * shards) * basis.T, coeffs.T + noise_q[ITERS - 1]


def solution(mesh):
    placed = (P("client", "shard", None), P(), P(None, "shard", None), P(None, "shard", None))
    return jax.shard_map(
        functools.partial(on_device, mesh.shape["client"], mesh.shape["shard"]),
        mesh=mesh,
        in_specs=placed,
        out_specs=(P("shard", None), P("shard", None)),
        check_vma=False,
    )
```
